32 devices in a mesh: groups: 2 (over x), tok: 16 (over z, y, core).
Axes of the slice: x: 2, y: 2, z: 4, core: 2. Of those that a mesh axis runs over, the one named last changes fastest.
Arguments:
- queries: bfloat16 [1024, 1024], P('tok'), may hold values from -64 to 64
- tokens: bfloat16 [32768, 1024], P(('groups', 'tok')), parts along dimension 0, may hold values from -6 to 6
- key_weight: bfloat16 [1024, 1024], replicated, may hold values from -1 to 1
- value_weight: bfloat16 [1024, 1024], replicated, may hold values from -0.1875 to 0.1875
- out_weight: bfloat16 [1024, 1024], replicated, may hold values from -0.1875 to 0.1875
Outputs:
- latent_update: bfloat16 [2048, 1024], P(('groups', 'tok')), parts along dimension 0
The draws below stay inside these ranges and needn't reach their ends.
There are 2 independent parts, one for each index of `groups`. The reference program is written for one: setup_inputs(seed, part) draws one part's arguments, and reference() takes and returns one part's arrays. A program takes and returns all parts, laid end to end along the dimension named above; an argument that names none is the same for every part. Nothing has to cross between parts.
All inputs are finite; a program needn't handle non-finite values.
Results may differ from the reference program's by a relative error of at most 0.0075.
The reference program's roundings to bfloat16 on the way (of `normed`, `key_rows`, `value_rows`, `probs` and `attended`) count: a program that leaves them out, or rounds other values in their place, can miss the bound.
Values may be sent and summed in bfloat16 or wider, within the bound.
A program may use at most 64 MiB of HBM per device.

```python
import math
import jax
import jax.numpy as jnp
from jax import lax

L = 1024
D = 1024
H = 16
HD = 64
TOKENS = 16384


def draw_queries(key, part):
    row_scale = jnp.exp(jax.random.uniform(jax.random.fold_in(key, 5), (L,), jnp.float32, math.log(2.0), math.log(5.0)))
    noise = jax.random.normal(jax.random.fold_in(key, 6), (L, D), jnp.float32)
    result = noise * row_scale[:, None]
    return jnp.clip(result, -64.0, 64.0).astype(jnp.bfloat16)


def draw_key_weight(key, part):
    base = jax.random.normal(jax.random.fold_in(key, 7), (D, D), jnp.float32) / math.sqrt(D)
    return jnp.clip(base, -1.0, 1.0).astype(jnp.bfloat16)


def block_levels(stream_key, dims, cuts, least, largest):
    gain, own = 1.0, jax.random.fold_in(stream_key, 6)
    for dim, shards_of in cuts:
        heights = jnp.exp(jax.random.uniform(jax.random.fold_in(own, dim), (shards_of,), jnp.float32, least / len(cuts), largest / len(cuts)))
        gain = gain * jnp.repeat(heights, dims[dim] // shards_of).reshape([-1 if axis == dim else 1 for axis in range(len(dims))])
    return gain


def centred(key, shape, width, reach, pieces=(), kind=jnp.bfloat16):
    drawn = width * jax.random.normal(key, shape, jnp.float32)
    if pieces:
        drawn = drawn * block_levels(key, shape, pieces, -0.22, 0.18)
    return jnp.clip(drawn, -reach, reach).astype(kind)


def setup_inputs(seed: int = 0, part: int = 0) -> dict:
    key_list = jax.random.split(jax.random.key(seed), 6)
    part_splits = jax.random.split(jax.random.fold_in(key_list[5], part), 6)
    queries = draw_queries(jax.random.fold_in(key_list[5], 71), part)
    tokens = centred(part_splits[1], (TOKENS, D), 1.0, 6.0, ((0, 16),))
    key_weight = draw_key_weight(jax.random.fold_in(key_list[5], 71), part)
    value_weight = centred(key_list[3], (D, D), D ** -0.5, 0.1875)
    out_weight = centred(key_list[4], (D, D), D ** -0.5, 0.1875)
    return dict(queries=queries, tokens=tokens, key_weight=key_weight, value_weight=value_weight, out_weight=out_weight)


epsilon = 1e-05

def layer_norm(matrix):
    widened = matrix.astype(jnp.float32)
    center = widened - lax.optimization_barrier(jnp.mean(widened, axis=1, keepdims=True))
    spread = lax.optimization_barrier(jnp.mean(center * center, axis=1, keepdims=True))
    return (center * lax.rsqrt(spread + epsilon)).astype(jnp.bfloat16)

def reference(queries, tokens, key_weight, value_weight, out_weight):
    normed = layer_norm(tokens)
    key_rows = jnp.dot(normed, key_weight, preferred_element_type=jnp.float32).astype(jnp.bfloat16)
    value_rows = jnp.dot(normed, value_weight, preferred_element_type=jnp.float32).astype(jnp.bfloat16)
    inverse_root = HD ** (-0.5)

    def one_head(head_index):
        first_col = (head_index * HD).astype(jnp.int32)
        head_query = lax.dynamic_slice_in_dim(queries, first_col, HD, 1)
        head_keys = lax.dynamic_slice_in_dim(key_rows, first_col, HD, 1)
        head_values = lax.dynamic_slice_in_dim(value_rows, first_col, HD, 1)
        scores = lax.dot_general(head_query, head_keys, (((1,), (1,)), ((), ())), preferred_element_type=jnp.float32) * inverse_root
        row_max = lax.optimization_barrier(jnp.max(scores, axis=1, keepdims=True))
        weights = jnp.exp(scores - row_max)
        totals = lax.optimization_barrier(jnp.sum(weights, axis=1, keepdims=True))
        probs = weights.astype(jnp.bfloat16)
        return jnp.dot(probs, head_values, preferred_element_type=jnp.float32) / totals
    stacked = lax.map(one_head, jnp.arange(H, dtype=jnp.int32))
    attended = jnp.transpose(stacked, (1, 0, 2)).reshape(L, H * HD).astype(jnp.bfloat16)
    return jnp.dot(attended, out_weight, preferred_element_type=jnp.float32).astype(jnp.bfloat16)
```

```python
import functools
import math

import jax
import jax.numpy as jnp
from jax import lax
from jax.experimental import pallas as pl
from jax.experimental.pallas import tpu as pltpu
from jax.sharding import PartitionSpec as P

H = 16
HD = 64


epsilon = 1e-05


def layer_norm(matrix):
    widened = matrix.astype(jnp.float32)
    center = widened - jnp.mean(widened, axis=1, keepdims=True)
    spread = jnp.mean(center * center, axis=1, keepdims=True)
    return (center * lax.rsqrt(spread + epsilon)).astype(jnp.bfloat16)


def head_partials(gathered, key_rows, value_rows, head_index):
    first_col = head_index * HD
    head_query = lax.dynamic_slice_in_dim(gathered, first_col, HD, 1)
    head_keys = lax.dynamic_slice_in_dim(key_rows, first_col, HD, 1)
    head_values = lax.dynamic_slice_in_dim(value_rows, first_col, HD, 1)
    scores = lax.dot_general(
        head_query, head_keys, (((1,), (1,)), ((), ())), preferred_element_type=jnp.float32
    ) * HD ** (-0.5)
    row_max = jnp.max(scores, axis=1)
    weights = jnp.exp(scores - row_max[:, None])
    totals = jnp.sum(weights, axis=1)
    partial_value = jnp.dot(
        weights.astype(jnp.bfloat16), head_values, preferred_element_type=jnp.float32
    )
    return (row_max, totals, partial_value)


def on_device(queries, tokens, key_weight, value_weight, out_weight):
    tok_count = lax.axis_size("tok")
    gathered = lax.all_gather(queries, "tok", axis=0, tiled=True)
    normed = layer_norm(tokens)
    key_rows = jnp.dot(normed, key_weight, preferred_element_type=jnp.float32).astype(jnp.bfloat16)
    value_rows = jnp.dot(normed, value_weight, preferred_element_type=jnp.float32).astype(
        jnp.bfloat16
    )

    def one_head(head_index):
        return head_partials(gathered, key_rows, value_rows, head_index)

    head_max, head_total, head_out = lax.map(one_head, jnp.arange(H, dtype=jnp.int32))
    latent_count = gathered.shape[0]
    owned_rows = latent_count // tok_count
    row_max = jnp.transpose(head_max)
    totals = jnp.transpose(head_total)
    partial_value = jnp.transpose(head_out, (1, 0, 2)).reshape(latent_count, H * HD)
    global_max = lax.pmax(row_max.astype(jnp.bfloat16), "tok").astype(row_max.dtype)
    factor = jnp.exp(row_max - global_max)
    scaled_out = (partial_value.reshape(latent_count, H, HD) * factor[..., None]).reshape(
        latent_count, H * HD
    )
    summed_out, summed_total = (
        lax.psum_scatter(scaled_out, "tok", scatter_dimension=0, tiled=True),
        lax.psum_scatter(totals * factor, "tok", scatter_dimension=0, tiled=True),
    )
    summed_out = summed_out.reshape(owned_rows, H, HD)
    attended = (
        (summed_out / summed_total[..., None]).reshape(owned_rows, H * HD).astype(jnp.bfloat16)
    )
    return jnp.dot(attended, out_weight, preferred_element_type=jnp.float32).astype(jnp.bfloat16)


GROUPS = 4
GH = H // GROUPS
GC = GH * HD
PAIRS = H // 2
GP = GH // 2
CHUNKS = 4
EXPO = math.log2(math.e) * HD ** (-0.5)


def fused(n, q_in, x_ref, wk_ref, wv_ref, wo_ref, out_ref,
          q_ref, k_ref, v_ref, acc_ref, st_ref, sbuf, rbuf, rst,
          att_ref, qs_sem, qr_sem, os_sem, or_sem, ts_sem, tr_sem):
    steps = n.bit_length() - 1
    rows = q_in.shape[0]
    tokens = x_ref.shape[0]
    me = lax.axis_index("tok")
    bits = [n >> (s + 1) for s in range(steps)]

    def partner(bit):
        return me + bit - 2 * bit * lax.rem(me // bit, 2)

    barrier = pltpu.get_barrier_semaphore()
    for bit in bits:
        pl.semaphore_signal(barrier, inc=1, device_id={"tok": partner(bit)}, device_id_type=pl.DeviceIdType.MESH)
    pl.semaphore_wait(barrier, steps)

    def gather(s):
        have = 1 << s
        return pltpu.make_async_remote_copy(
            src_ref=q_ref.at[pl.ds(0, have)], dst_ref=q_ref.at[pl.ds(have, have)],
            send_sem=qs_sem.at[s], recv_sem=qr_sem.at[s],
            device_id={"tok": partner(n >> (s + 1))}, device_id_type=pl.DeviceIdType.MESH)

    def reduce_out(g, s):
        half = n >> (s + 1)
        return pltpu.make_async_remote_copy(
            src_ref=sbuf.at[g, pl.ds(half, half)], dst_ref=rbuf.at[g, pl.ds(half, half)],
            send_sem=os_sem.at[g, s], recv_sem=or_sem.at[g, s],
            device_id={"tok": partner(1 << s)}, device_id_type=pl.DeviceIdType.MESH)

    def reduce_stat(g, s):
        half = n >> (s + 1)
        return pltpu.make_async_remote_copy(
            src_ref=st_ref.at[g, pl.ds(half, half)], dst_ref=rst.at[g, pl.ds(half, half)],
            send_sem=ts_sem.at[g, s], recv_sem=tr_sem.at[g, s],
            device_id={"tok": partner(1 << s)}, device_id_type=pl.DeviceIdType.MESH)

    q_ref[0] = q_in[...]
    gather(0).start()

    part = tokens // CHUNKS

    def project(c):
        first = c * part
        x = x_ref[pl.ds(first, part), :].astype(jnp.float32)
        center = x - jnp.mean(x, axis=1, keepdims=True)
        spread = jnp.mean(center * center, axis=1, keepdims=True)
        normed = (center * lax.rsqrt(spread + epsilon)).astype(jnp.bfloat16)
        ones = jnp.ones((part, 2 * HD), jnp.bfloat16)
        keys = jnp.dot(normed, wk_ref[...], preferred_element_type=jnp.float32).astype(jnp.bfloat16)
        for p in range(PAIRS):
            k_ref[p, pl.ds(first, part), :] = keys[:, p * 128 : (p + 1) * 128]
        values = jnp.dot(normed, wv_ref[...], preferred_element_type=jnp.float32).astype(jnp.bfloat16)
        for p in range(PAIRS):
            v_ref[p, pl.ds(first, part), 0:128] = values[:, p * 128 : (p + 1) * 128]
            v_ref[p, pl.ds(first, part), 128:256] = ones

    def project_some(first, last):
        @pl.loop(first, last)
        def _(c):
            project(c)

    project_some(0, CHUNKS // 2)
    gather(0).wait_recv()
    gather(1).start()
    project_some(CHUNKS // 2, CHUNKS)
    gather(1).wait_recv()
    gather(2).start()

    quarter = n // 4
    chunk = quarter * rows
    lane = lax.broadcasted_iota(jnp.int32, (chunk, 128), 1)

    def attend(g, q):
        stats = jnp.zeros((chunk, 128), jnp.float32)
        for j in range(GP):
            pair = g * GP + j
            cols = pl.ds(pl.multiple_of(pair * 128, 128), 128)
            query = q_ref[pl.ds(q * quarter, quarter), :, cols].reshape(chunk, 128)
            zero = jnp.zeros_like(query)
            both = jnp.concatenate([jnp.where(lane < HD, query, zero), jnp.where(lane < HD, zero, query)], axis=0)
            scores = lax.dot_general(both, k_ref[pair], (((1,), (1,)), ((), ())), preferred_element_type=jnp.float32)
            top = jnp.max(scores, axis=1, keepdims=True)
            weights = jnp.exp2((scores - top) * EXPO).astype(jnp.bfloat16)
            product = jnp.dot(weights, v_ref[pair], preferred_element_type=jnp.float32)
            merged = jnp.where(lane < HD, product[:chunk, :128], product[chunk:, :128]).reshape(quarter, rows, 128)
            where = slice(j * 128, (j + 1) * 128)
            if q < 2:
                acc_ref[g, pl.ds(q * quarter, quarter), :, where] = merged
            else:
                sbuf[g, pl.ds(q * quarter, quarter), :, where] = merged.astype(jnp.bfloat16)
            for e in range(2):
                mine = slice(e * chunk, (e + 1) * chunk)
                stats = jnp.where(lane == 2 * j + e, top[mine], stats)
                stats = jnp.where(lane == GH + 2 * j + e, product[mine, 128:], stats)
        for b in range(quarter):
            turned = stats[b * rows : (b + 1) * rows].T
            st_ref[g, q * quarter + b] = turned[: 2 * GH]

    narrow = lax.broadcasted_iota(jnp.int32, (rows, 128), 1) < HD

    def spread_heads(turned):
        return jnp.concatenate(
            [jnp.where(narrow, turned[:, 2 * j : 2 * j + 1], turned[:, 2 * j + 1 : 2 * j + 2]) for j in range(GP)], axis=1)

    def combine(g, s):
        half = n >> (s + 1)
        reduce_out(g, s).wait_recv()
        reduce_stat(g, s).wait_recv()

        def one(b):
            own, other = st_ref[g, b], rst[g, half + b]
            top = jnp.maximum(own[:GH], other[:GH])
            f_own = jnp.exp2((own[:GH] - top) * EXPO)
            f_other = jnp.exp2((other[:GH] - top) * EXPO)
            total = own[GH:] * f_own + other[GH:] * f_other
            st_ref[g, b] = jnp.concatenate([top, total], axis=0)
            turned = jnp.concatenate([f_own, f_other], axis=0).T
            summed = (acc_ref[g, b] * spread_heads(turned[:, :GH])
                      + rbuf[g, half + b].astype(jnp.float32) * spread_heads(turned[:, GH:]))
            return summed

        for b in range(half):
            summed = one(b)
            if b >= half // 2 and half > 1:
                sbuf[g, b] = summed.astype(jnp.bfloat16)
            else:
                acc_ref[g, b] = summed
        if s + 1 < steps:
            reduce_out(g, s + 1).start()
            reduce_stat(g, s + 1).start()

    @pl.loop(0, GROUPS)
    def _(g):
        for q in range(4):
            if q in (1, 2):
                @pl.when(g == 0)
                def _():
                    gather(q + 1).wait_recv()
                    if q + 2 < steps:
                        gather(q + 2).start()
            attend(g, q)
            if q == 3:
                reduce_out(g, 0).start()
                reduce_stat(g, 0).start()

            @pl.when(g > 0)
            def _():
                combine(g - 1, q)

    for s in range(steps):
        combine(GROUPS - 1, s)

    for g in range(GROUPS):
        share = spread_heads(st_ref[g, 0].T[:, GH:])
        att_ref[:, g * GC : (g + 1) * GC] = (acc_ref[g, 0] / share).astype(jnp.bfloat16)
    out_ref[...] = jnp.dot(att_ref[...], wo_ref[...], preferred_element_type=jnp.float32).astype(out_ref.dtype)

    for s in range(steps):
        gather(s).wait_send()

    @pl.loop(0, GROUPS)
    def _(g):
        for s in range(steps):
            reduce_out(g, s).wait_send()
            reduce_stat(g, s).wait_send()


def program(queries, tokens, key_weight, value_weight, out_weight):
    n = lax.axis_size("tok")
    rows, width = queries.shape
    count = tokens.shape[0]
    if n != 16 or rows % 16 or count % 1024 or width != H * HD:
        return on_device(queries, tokens, key_weight, value_weight, out_weight)
    vmem = pl.BlockSpec(memory_space=pltpu.VMEM)
    steps = n.bit_length() - 1
    return pl.pallas_call(
        functools.partial(fused, n),
        out_shape=jax.ShapeDtypeStruct((rows, width), jnp.bfloat16),
        in_specs=[vmem] * 5,
        out_specs=vmem,
        scratch_shapes=[
            pltpu.VMEM((n, rows, width), jnp.bfloat16),
            pltpu.VMEM((PAIRS, count, 128), jnp.bfloat16),
            pltpu.VMEM((PAIRS, count, 256), jnp.bfloat16),
            pltpu.VMEM((GROUPS, n // 2, rows, GC), jnp.float32),
            pltpu.VMEM((GROUPS, n, 2 * GH, rows), jnp.float32),
            pltpu.VMEM((GROUPS, n, rows, GC), jnp.bfloat16),
            pltpu.VMEM((GROUPS, n, rows, GC), jnp.bfloat16),
            pltpu.VMEM((GROUPS, n, 2 * GH, rows), jnp.float32),
            pltpu.VMEM((rows, width), jnp.bfloat16),
            pltpu.SemaphoreType.DMA((steps,)),
            pltpu.SemaphoreType.DMA((steps,)),
            pltpu.SemaphoreType.DMA((GROUPS, steps)),
            pltpu.SemaphoreType.DMA((GROUPS, steps)),
            pltpu.SemaphoreType.DMA((GROUPS, steps)),
            pltpu.SemaphoreType.DMA((GROUPS, steps)),
        ],
        compiler_params=pltpu.CompilerParams(
            collective_id=0, has_side_effects=True, vmem_limit_bytes=56 * 2**20),
    )(queries, tokens, key_weight, value_weight, out_weight)


def solution(mesh):
    placed = (P("tok", None), P(("groups", "tok"), None), P(), P(), P())
    return jax.shard_map(
        program, mesh=mesh, in_specs=placed, out_specs=P(("groups", "tok"), None), check_vma=False
    )
```

```python
import functools
import math

import jax
import jax.numpy as jnp
from jax import lax
from jax.experimental import pallas as pl
from jax.experimental.pallas import tpu as pltpu
from jax.sharding import PartitionSpec as P

H = 16
HD = 64


epsilon = 1e-05


def layer_norm(matrix):
    widened = matrix.astype(jnp.float32)
    center = widened - jnp.mean(widened, axis=1, keepdims=True)
    spread = jnp.mean(center * center, axis=1, keepdims=True)
    return (center * lax.rsqrt(spread + epsilon)).astype(jnp.bfloat16)


def head_partials(gathered, key_rows, value_rows, head_index):
    first_col = head_index * HD
    head_query = lax.dynamic_slice_in_dim(gathered, first_col, HD, 1)
    head_keys = lax.dynamic_slice_in_dim(key_rows, first_col, HD, 1)
    head_values = lax.dynamic_slice_in_dim(value_rows, first_col, HD, 1)
    scores = lax.dot_general(
        head_query, head_keys, (((1,), (1,)), ((), ())), preferred_element_type=jnp.float32
    ) * HD ** (-0.5)
    row_max = jnp.max(scores, axis=1)
    weights = jnp.exp(scores - row_max[:, None])
    totals = jnp.sum(weights, axis=1)
    partial_value = jnp.dot(
        weights.astype(jnp.bfloat16), head_values, preferred_element_type=jnp.float32
    )
    return (row_max, totals, partial_value)


def on_device(queries, tokens, key_weight, value_weight, out_weight):
    tok_count = lax.axis_size("tok")
    gathered = lax.all_gather(queries, "tok", axis=0, tiled=True)
    normed = layer_norm(tokens)
    key_rows = jnp.dot(normed, key_weight, preferred_element_type=jnp.float32).astype(jnp.bfloat16)
    value_rows = jnp.dot(normed, value_weight, preferred_element_type=jnp.float32).astype(
        jnp.bfloat16
    )

    def one_head(head_index):
        return head_partials(gathered, key_rows, value_rows, head_index)

    head_max, head_total, head_out = lax.map(one_head, jnp.arange(H, dtype=jnp.int32))
    latent_count = gathered.shape[0]
    owned_rows = latent_count // tok_count
    row_max = jnp.transpose(head_max)
    totals = jnp.transpose(head_total)
    partial_value = jnp.transpose(head_out, (1, 0, 2)).reshape(latent_count, H * HD)
    global_max = lax.pmax(row_max.astype(jnp.bfloat16), "tok").astype(row_max.dtype)
    factor = jnp.exp(row_max - global_max)
    scaled_out = (partial_value.reshape(latent_count, H, HD) * factor[..., None]).reshape(
        latent_count, H * HD
    )
    summed_out, summed_total = (
        lax.psum_scatter(scaled_out, "tok", scatter_dimension=0, tiled=True),
        lax.psum_scatter(totals * factor, "tok", scatter_dimension=0, tiled=True),
    )
    summed_out = summed_out.reshape(owned_rows, H, HD)
    attended = (
        (summed_out / summed_total[..., None]).reshape(owned_rows, H * HD).astype(jnp.bfloat16)
    )
    return jnp.dot(attended, out_weight, preferred_element_type=jnp.float32).astype(jnp.bfloat16)


GROUPS = 4
GH = H // GROUPS
GC = GH * HD
PAIRS = H // 2
GP = GH // 2
CHUNKS = 4
EXPO = math.log2(math.e) * HD ** (-0.5)


def fused(n, q_in, x_in, wk_in, wv_in, wo_in, out_ref,
          x_ref, wk_ref, wv_ref, wo_ref, load_sem,
          q_ref, k_ref, v_ref, acc_ref, st_ref, sbuf, rbuf, rst,
          att_ref, qs_sem, qr_sem, os_sem, or_sem, ts_sem, tr_sem):
    steps = n.bit_length() - 1
    rows = q_in.shape[0]
    tokens = x_ref.shape[0]
    me = lax.axis_index("tok")
    bits = [n >> (s + 1) for s in range(steps)]

    def partner(bit):
        return me + bit - 2 * bit * lax.rem(me // bit, 2)

    loads = [
        pltpu.make_async_copy(src, dst, load_sem.at[i])
        for i, (src, dst) in enumerate(((x_in, x_ref), (wk_in, wk_ref), (wv_in, wv_ref), (wo_in, wo_ref)))]
    barrier = pltpu.get_barrier_semaphore()
    for bit in bits:
        pl.semaphore_signal(barrier, inc=1, device_id={"tok": partner(bit)}, device_id_type=pl.DeviceIdType.MESH)
    for load in loads:
        load.start()
    q_ref[0] = q_in[...]
    pl.semaphore_wait(barrier, steps)

    def gather(s):
        have = 1 << s
        return pltpu.make_async_remote_copy(
            src_ref=q_ref.at[pl.ds(0, have)], dst_ref=q_ref.at[pl.ds(have, have)],
            send_sem=qs_sem.at[s], recv_sem=qr_sem.at[s],
            device_id={"tok": partner(n >> (s + 1))}, device_id_type=pl.DeviceIdType.MESH)

    def reduce_out(g, s):
        half = n >> (s + 1)
        return pltpu.make_async_remote_copy(
            src_ref=sbuf.at[g, pl.ds(half, half)], dst_ref=rbuf.at[g, pl.ds(half, half)],
            send_sem=os_sem.at[g, s], recv_sem=or_sem.at[g, s],
            device_id={"tok": partner(1 << s)}, device_id_type=pl.DeviceIdType.MESH)

    def reduce_stat(g, s):
        half = n >> (s + 1)
        return pltpu.make_async_remote_copy(
            src_ref=st_ref.at[g, pl.ds(half, half)], dst_ref=rst.at[g, pl.ds(half, half)],
            send_sem=ts_sem.at[g, s], recv_sem=tr_sem.at[g, s],
            device_id={"tok": partner(1 << s)}, device_id_type=pl.DeviceIdType.MESH)

    gather(0).start()

    part = tokens // CHUNKS

    def project(c):
        first = c * part
        x = x_ref[pl.ds(first, part), :].astype(jnp.float32)
        center = x - jnp.mean(x, axis=1, keepdims=True)
        spread = jnp.mean(center * center, axis=1, keepdims=True)
        normed = (center * lax.rsqrt(spread + epsilon)).astype(jnp.bfloat16)
        ones = jnp.ones((part, 2 * HD), jnp.bfloat16)
        keys = jnp.dot(normed, wk_ref[...], preferred_element_type=jnp.float32).astype(jnp.bfloat16)
        for p in range(PAIRS):
            k_ref[p, pl.ds(first, part), :] = keys[:, p * 128 : (p + 1) * 128]
        values = jnp.dot(normed, wv_ref[...], preferred_element_type=jnp.float32).astype(jnp.bfloat16)
        for p in range(PAIRS):
            v_ref[p, pl.ds(first, part), 0:128] = values[:, p * 128 : (p + 1) * 128]
            v_ref[p, pl.ds(first, part), 128:256] = ones

    def project_some(first, last):
        @pl.loop(first, last)
        def _(c):
            project(c)

    for load in loads[:3]:
        load.wait()
    project_some(0, CHUNKS // 2)
    gather(0).wait_recv()
    gather(1).start()
    project_some(CHUNKS // 2, CHUNKS)
    gather(1).wait_recv()
    gather(2).start()

    quarter = n // 4
    chunk = quarter * rows
    lane = lax.broadcasted_iota(jnp.int32, (chunk, 128), 1)

    def attend(g, q):
        stats = jnp.zeros((chunk, 128), jnp.float32)
        for j in range(GP):
            pair = g * GP + j
            cols = pl.ds(pl.multiple_of(pair * 128, 128), 128)
            query = q_ref[pl.ds(q * quarter, quarter), :, cols].reshape(chunk, 128)
            zero = jnp.zeros_like(query)
            both = jnp.concatenate([jnp.where(lane < HD, query, zero), jnp.where(lane < HD, zero, query)], axis=0)
            scores = lax.dot_general(both, k_ref[pair], (((1,), (1,)), ((), ())), preferred_element_type=jnp.float32)
            top = jnp.max(scores, axis=1, keepdims=True)
            weights = jnp.exp2((scores - top) * EXPO).astype(jnp.bfloat16)
            product = jnp.dot(weights, v_ref[pair], preferred_element_type=jnp.float32)
            merged = jnp.where(lane < HD, product[:chunk, :128], product[chunk:, :128]).reshape(quarter, rows, 128)
            where = slice(j * 128, (j + 1) * 128)
            if q < 2:
                acc_ref[g, pl.ds(q * quarter, quarter), :, where] = merged
            else:
                sbuf[g, pl.ds(q * quarter, quarter), :, where] = merged.astype(jnp.bfloat16)
            for e in range(2):
                mine = slice(e * chunk, (e + 1) * chunk)
                stats = jnp.where(lane == 2 * j + e, top[mine], stats)
                stats = jnp.where(lane == GH + 2 * j + e, product[mine, 128:], stats)
        for b in range(quarter):
            turned = stats[b * rows : (b + 1) * rows].T
            st_ref[g, q * quarter + b] = turned[: 2 * GH]

    narrow = lax.broadcasted_iota(jnp.int32, (rows, 128), 1) < HD

    def spread_heads(turned):
        return jnp.concatenate(
            [jnp.where(narrow, turned[:, 2 * j : 2 * j + 1], turned[:, 2 * j + 1 : 2 * j + 2]) for j in range(GP)], axis=1)

    def combine(g, s):
        half = n >> (s + 1)
        reduce_out(g, s).wait_recv()
        reduce_stat(g, s).wait_recv()

        def one(b):
            own, other = st_ref[g, b], rst[g, half + b]
            top = jnp.maximum(own[:GH], other[:GH])
            f_own = jnp.exp2((own[:GH] - top) * EXPO)
            f_other = jnp.exp2((other[:GH] - top) * EXPO)
            total = own[GH:] * f_own + other[GH:] * f_other
            st_ref[g, b] = jnp.concatenate([top, total], axis=0)
            turned = jnp.concatenate([f_own, f_other], axis=0).T
            summed = (acc_ref[g, b] * spread_heads(turned[:, :GH])
                      + rbuf[g, half + b].astype(jnp.float32) * spread_heads(turned[:, GH:]))
            return summed

        for b in range(half):
            summed = one(b)
            if b >= half // 2 and half > 1:
                sbuf[g, b] = summed.astype(jnp.bfloat16)
            else:
                acc_ref[g, b] = summed
        if s + 1 < steps:
            reduce_out(g, s + 1).start()
            reduce_stat(g, s + 1).start()

    @pl.loop(0, GROUPS)
    def _(g):
        attend(g, 0)

    gather(2).wait_recv()
    gather(3).start()

    @pl.loop(0, GROUPS)
    def _(g):
        attend(g, 1)

    gather(3).wait_recv()

    @pl.loop(0, GROUPS)
    def _(g):
        attend(g, 2)
        attend(g, 3)
        reduce_out(g, 0).start()
        reduce_stat(g, 0).start()
        for s in reversed(range(min(steps, GROUPS - 1))):
            @pl.when(g > s)
            def _():
                combine(g - 1 - s, s)

    for t in range(GROUPS, GROUPS + steps):
        for s in reversed(range(steps)):
            if 0 <= t - 1 - s < GROUPS:
                combine(t - 1 - s, s)

    for g in range(GROUPS):
        share = spread_heads(st_ref[g, 0].T[:, GH:])
        att_ref[:, g * GC : (g + 1) * GC] = (acc_ref[g, 0] / share).astype(jnp.bfloat16)
    loads[3].wait()
    out_ref[...] = jnp.dot(att_ref[...], wo_ref[...], preferred_element_type=jnp.float32).astype(out_ref.dtype)

    for s in range(steps):
        gather(s).wait_send()

    @pl.loop(0, GROUPS)
    def _(g):
        for s in range(steps):
            reduce_out(g, s).wait_send()
            reduce_stat(g, s).wait_send()


def program(queries, tokens, key_weight, value_weight, out_weight):
    n = lax.axis_size("tok")
    rows, width = queries.shape
    count = tokens.shape[0]
    if n != 16 or rows % 16 or count % 1024 or width != H * HD:
        return on_device(queries, tokens, key_weight, value_weight, out_weight)
    vmem = pl.BlockSpec(memory_space=pltpu.VMEM)
    steps = n.bit_length() - 1
    return pl.pallas_call(
        functools.partial(fused, n),
        out_shape=jax.ShapeDtypeStruct((rows, width), jnp.bfloat16),
        in_specs=[vmem] + [pl.BlockSpec(memory_space=pl.ANY)] * 4,
        out_specs=vmem,
        scratch_shapes=[
            pltpu.VMEM(tokens.shape, tokens.dtype),
            pltpu.VMEM(key_weight.shape, key_weight.dtype),
            pltpu.VMEM(value_weight.shape, value_weight.dtype),
            pltpu.VMEM(out_weight.shape, out_weight.dtype),
            pltpu.SemaphoreType.DMA((4,)),
            pltpu.VMEM((n, rows, width), jnp.bfloat16),
            pltpu.VMEM((PAIRS, count, 128), jnp.bfloat16),
            pltpu.VMEM((PAIRS, count, 256), jnp.bfloat16),
            pltpu.VMEM((GROUPS, n // 2, rows, GC), jnp.float32),
            pltpu.VMEM((GROUPS, n, 2 * GH, rows), jnp.float32),
            pltpu.VMEM((GROUPS, n, rows, GC), jnp.bfloat16),
            pltpu.VMEM((GROUPS, n, rows, GC), jnp.bfloat16),
            pltpu.VMEM((GROUPS, n, 2 * GH, rows), jnp.float32),
            pltpu.VMEM((rows, width), jnp.bfloat16),
            pltpu.SemaphoreType.DMA((steps,)),
            pltpu.SemaphoreType.DMA((steps,)),
            pltpu.SemaphoreType.DMA((GROUPS, steps)),
            pltpu.SemaphoreType.DMA((GROUPS, steps)),
            pltpu.SemaphoreType.DMA((GROUPS, steps)),
            pltpu.SemaphoreType.DMA((GROUPS, steps)),
        ],
        compiler_params=pltpu.CompilerParams(
            collective_id=0, has_side_effects=True, vmem_limit_bytes=56 * 2**20),
    )(queries, tokens, key_weight, value_weight, out_weight)


def solution(mesh):
    placed = (P("tok", None), P(("groups", "tok"), None), P(), P(), P())
    return jax.shard_map(
        program, mesh=mesh, in_specs=placed, out_specs=P(("groups", "tok"), None), check_vma=False
    )
```

```python
import functools
import math

import jax
import jax.numpy as jnp
from jax import lax
from jax.experimental import pallas as pl
from jax.experimental.pallas import tpu as pltpu
from jax.sharding import PartitionSpec as P

H = 16
HD = 64


epsilon = 1e-05


def layer_norm(matrix):
    widened = matrix.astype(jnp.float32)
    center = widened - jnp.mean(widened, axis=1, keepdims=True)
    spread = jnp.mean(center * center, axis=1, keepdims=True)
    return (center * lax.rsqrt(spread + epsilon)).astype(jnp.bfloat16)


def head_partials(gathered, key_rows, value_rows, head_index):
    first_col = head_index * HD
    head_query = lax.dynamic_slice_in_dim(gathered, first_col, HD, 1)
    head_keys = lax.dynamic_slice_in_dim(key_rows, first_col, HD, 1)
    head_values = lax.dynamic_slice_in_dim(value_rows, first_col, HD, 1)
    scores = lax.dot_general(
        head_query, head_keys, (((1,), (1,)), ((), ())), preferred_element_type=jnp.float32
    ) * HD ** (-0.5)
    row_max = jnp.max(scores, axis=1)
    weights = jnp.exp(scores - row_max[:, None])
    totals = jnp.sum(weights, axis=1)
    partial_value = jnp.dot(
        weights.astype(jnp.bfloat16), head_values, preferred_element_type=jnp.float32
    )
    return (row_max, totals, partial_value)


def on_device(queries, tokens, key_weight, value_weight, out_weight):
    tok_count = lax.axis_size("tok")
    gathered = lax.all_gather(queries, "tok", axis=0, tiled=True)
    normed = layer_norm(tokens)
    key_rows = jnp.dot(normed, key_weight, preferred_element_type=jnp.float32).astype(jnp.bfloat16)
    value_rows = jnp.dot(normed, value_weight, preferred_element_type=jnp.float32).astype(
        jnp.bfloat16
    )

    def one_head(head_index):
        return head_partials(gathered, key_rows, value_rows, head_index)

    head_max, head_total, head_out = lax.map(one_head, jnp.arange(H, dtype=jnp.int32))
    latent_count = gathered.shape[0]
    owned_rows = latent_count // tok_count
    row_max = jnp.transpose(head_max)
    totals = jnp.transpose(head_total)
    partial_value = jnp.transpose(head_out, (1, 0, 2)).reshape(latent_count, H * HD)
    global_max = lax.pmax(row_max.astype(jnp.bfloat16), "tok").astype(row_max.dtype)
    factor = jnp.exp(row_max - global_max)
    scaled_out = (partial_value.reshape(latent_count, H, HD) * factor[..., None]).reshape(
        latent_count, H * HD
    )
    summed_out, summed_total = (
        lax.psum_scatter(scaled_out, "tok", scatter_dimension=0, tiled=True),
        lax.psum_scatter(totals * factor, "tok", scatter_dimension=0, tiled=True),
    )
    summed_out = summed_out.reshape(owned_rows, H, HD)
    attended = (
        (summed_out / summed_total[..., None]).reshape(owned_rows, H * HD).astype(jnp.bfloat16)
    )
    return jnp.dot(attended, out_weight, preferred_element_type=jnp.float32).astype(jnp.bfloat16)


GROUPS = 4
GH = H // GROUPS
GC = GH * HD
PAIRS = H // 2
GP = GH // 2
CHUNKS = 4
EXPO = math.log2(math.e) * HD ** (-0.5)


def fused(n, q_in, x_in, wk_in, wv_in, wo_in, out_ref,
          x_ref, wk_ref, wv_ref, wo_ref, load_sem,
          q_ref, k_ref, v_ref, acc_ref, st_ref, sbuf, rbuf, rst,
          att_ref, qs_sem, qr_sem, os_sem, or_sem, ts_sem, tr_sem):
    steps = n.bit_length() - 1
    rows = q_in.shape[0]
    tokens = x_ref.shape[0]
    me = lax.axis_index("tok")
    bits = [n >> (s + 1) for s in range(steps)]

    def partner(bit):
        return me + bit - 2 * bit * lax.rem(me // bit, 2)

    loads = [
        pltpu.make_async_copy(src, dst, load_sem.at[i])
        for i, (src, dst) in enumerate(((x_in, x_ref), (wk_in, wk_ref), (wv_in, wv_ref), (wo_in, wo_ref)))]
    barrier = pltpu.get_barrier_semaphore()
    for bit in bits:
        pl.semaphore_signal(barrier, inc=1, device_id={"tok": partner(bit)}, device_id_type=pl.DeviceIdType.MESH)
    for load in loads:
        load.start()
    q_ref[0] = q_in[...]
    pl.semaphore_wait(barrier, steps)

    def gather(s, part):
        first = 0 if part == 0 else 1 << (part - 1)
        size = max(first, 1)
        return pltpu.make_async_remote_copy(
            src_ref=q_ref.at[pl.ds(first, size)], dst_ref=q_ref.at[pl.ds((1 << s) + first, size)],
            send_sem=qs_sem.at[s, part], recv_sem=qr_sem.at[s, part],
            device_id={"tok": partner(n >> (s + 1))}, device_id_type=pl.DeviceIdType.MESH)

    def arrived(k):
        for part in range(k + 1):
            gather(k, part).wait_recv()
        for s in range(k + 1, steps):
            gather(s, k + 1).start()

    def reduce_out(g, s):
        half = n >> (s + 1)
        return pltpu.make_async_remote_copy(
            src_ref=sbuf.at[g, pl.ds(half, half)], dst_ref=rbuf.at[g, pl.ds(half, half)],
            send_sem=os_sem.at[g, s], recv_sem=or_sem.at[g, s],
            device_id={"tok": partner(1 << s)}, device_id_type=pl.DeviceIdType.MESH)

    def reduce_stat(g, s):
        half = n >> (s + 1)
        return pltpu.make_async_remote_copy(
            src_ref=st_ref.at[g, pl.ds(half, half)], dst_ref=rst.at[g, pl.ds(half, half)],
            send_sem=ts_sem.at[g, s], recv_sem=tr_sem.at[g, s],
            device_id={"tok": partner(1 << s)}, device_id_type=pl.DeviceIdType.MESH)

    for s in range(steps):
        gather(s, 0).start()

    part = tokens // CHUNKS

    def project(c):
        first = c * part
        x = x_ref[pl.ds(first, part), :].astype(jnp.float32)
        center = x - jnp.mean(x, axis=1, keepdims=True)
        spread = jnp.mean(center * center, axis=1, keepdims=True)
        normed = (center * lax.rsqrt(spread + epsilon)).astype(jnp.bfloat16)
        ones = jnp.ones((part, 2 * HD), jnp.bfloat16)
        keys = jnp.dot(normed, wk_ref[...], preferred_element_type=jnp.float32).astype(jnp.bfloat16)
        for p in range(PAIRS):
            k_ref[p, pl.ds(first, part), :] = keys[:, p * 128 : (p + 1) * 128]
        values = jnp.dot(normed, wv_ref[...], preferred_element_type=jnp.float32).astype(jnp.bfloat16)
        for p in range(PAIRS):
            v_ref[p, pl.ds(first, part), 0:128] = values[:, p * 128 : (p + 1) * 128]
            v_ref[p, pl.ds(first, part), 128:256] = ones

    def project_some(first, last):
        @pl.loop(first, last)
        def _(c):
            project(c)

    for load in loads[:3]:
        load.wait()
    project_some(0, CHUNKS - 1)
    arrived(0)
    project_some(CHUNKS - 1, CHUNKS)
    arrived(1)

    quarter = n // 4
    chunk = quarter * rows
    lane = lax.broadcasted_iota(jnp.int32, (chunk, 128), 1)

    def attend(g, q):
        stats = jnp.zeros((chunk, 128), jnp.float32)
        for j in range(GP):
            pair = g * GP + j
            cols = pl.ds(pl.multiple_of(pair * 128, 128), 128)
            query = q_ref[pl.ds(q * quarter, quarter), :, cols].reshape(chunk, 128)
            zero = jnp.zeros_like(query)
            both = jnp.concatenate([jnp.where(lane < HD, query, zero), jnp.where(lane < HD, zero, query)], axis=0)
            scores = lax.dot_general(both, k_ref[pair], (((1,), (1,)), ((), ())), preferred_element_type=jnp.float32)
            top = jnp.max(scores, axis=1, keepdims=True)
            weights = jnp.exp2((scores - top) * EXPO).astype(jnp.bfloat16)
            product = jnp.dot(weights, v_ref[pair], preferred_element_type=jnp.float32)
            merged = jnp.where(lane < HD, product[:chunk, :128], product[chunk:, :128]).reshape(quarter, rows, 128)
            where = slice(j * 128, (j + 1) * 128)
            if q < 2:
                acc_ref[g, pl.ds(q * quarter, quarter), :, where] = merged
            else:
                sbuf[g, pl.ds(q * quarter, quarter), :, where] = merged.astype(jnp.bfloat16)
            for e in range(2):
                mine = slice(e * chunk, (e + 1) * chunk)
                stats = jnp.where(lane == 2 * j + e, top[mine], stats)
                stats = jnp.where(lane == GH + 2 * j + e, product[mine, 128:], stats)
        for b in range(quarter):
            turned = stats[b * rows : (b + 1) * rows].T
            st_ref[g, q * quarter + b] = turned[: 2 * GH]

    narrow = lax.broadcasted_iota(jnp.int32, (rows, 128), 1) < HD

    def spread_heads(turned):
        return jnp.concatenate(
            [jnp.where(narrow, turned[:, 2 * j : 2 * j + 1], turned[:, 2 * j + 1 : 2 * j + 2]) for j in range(GP)], axis=1)

    def combine(g, s):
        half = n >> (s + 1)
        reduce_out(g, s).wait_recv()
        reduce_stat(g, s).wait_recv()

        def one(b):
            own, other = st_ref[g, b], rst[g, half + b]
            top = jnp.maximum(own[:GH], other[:GH])
            f_own = jnp.exp2((own[:GH] - top) * EXPO)
            f_other = jnp.exp2((other[:GH] - top) * EXPO)
            total = own[GH:] * f_own + other[GH:] * f_other
            st_ref[g, b] = jnp.concatenate([top, total], axis=0)
            turned = jnp.concatenate([f_own, f_other], axis=0).T
            summed = (acc_ref[g, b] * spread_heads(turned[:, :GH])
                      + rbuf[g, half + b].astype(jnp.float32) * spread_heads(turned[:, GH:]))
            return summed

        for b in range(half):
            summed = one(b)
            if b >= half // 2 and half > 1:
                sbuf[g, b] = summed.astype(jnp.bfloat16)
            else:
                acc_ref[g, b] = summed
        if s + 1 < steps:
            reduce_out(g, s + 1).start()
            reduce_stat(g, s + 1).start()

    @pl.loop(0, GROUPS)
    def _(g):
        attend(g, 0)

    arrived(2)

    @pl.loop(0, GROUPS - 1)
    def _(g):
        attend(g, 1)

    arrived(3)

    @pl.loop(0, GROUPS)
    def _(g):
        attend(g, 2)
        attend(g, 3)
        reduce_out(g, 0).start()
        reduce_stat(g, 0).start()
        for s in reversed(range(min(steps, GROUPS - 1))):
            @pl.when(g > s)
            def _():
                combine(g - 1 - s, s)

    attend(GROUPS - 1, 1)
    for t in range(GROUPS, GROUPS + steps):
        for s in reversed(range(steps)):
            if 0 <= t - 1 - s < GROUPS:
                combine(t - 1 - s, s)

    for g in range(GROUPS):
        share = spread_heads(st_ref[g, 0].T[:, GH:])
        att_ref[:, g * GC : (g + 1) * GC] = (acc_ref[g, 0] / share).astype(jnp.bfloat16)
    loads[3].wait()
    out_ref[...] = jnp.dot(att_ref[...], wo_ref[...], preferred_element_type=jnp.float32).astype(out_ref.dtype)

    for s in range(steps):
        for part in range(s + 1):
            gather(s, part).wait_send()

    @pl.loop(0, GROUPS)
    def _(g):
        for s in range(steps):
            reduce_out(g, s).wait_send()
            reduce_stat(g, s).wait_send()


def program(queries, tokens, key_weight, value_weight, out_weight):
    n = lax.axis_size("tok")
    rows, width = queries.shape
    count = tokens.shape[0]
    if n != 16 or rows % 16 or count % 1024 or width != H * HD:
        return on_device(queries, tokens, key_weight, value_weight, out_weight)
    vmem = pl.BlockSpec(memory_space=pltpu.VMEM)
    steps = n.bit_length() - 1
    return pl.pallas_call(
        functools.partial(fused, n),
        out_shape=jax.ShapeDtypeStruct((rows, width), jnp.bfloat16),
        in_specs=[vmem] + [pl.BlockSpec(memory_space=pl.ANY)] * 4,
        out_specs=vmem,
        scratch_shapes=[
            pltpu.VMEM(tokens.shape, tokens.dtype),
            pltpu.VMEM(key_weight.shape, key_weight.dtype),
            pltpu.VMEM(value_weight.shape, value_weight.dtype),
            pltpu.VMEM(out_weight.shape, out_weight.dtype),
            pltpu.SemaphoreType.DMA((4,)),
            pltpu.VMEM((n, rows, width), jnp.bfloat16),
            pltpu.VMEM((PAIRS, count, 128), jnp.bfloat16),
            pltpu.VMEM((PAIRS, count, 256), jnp.bfloat16),
            pltpu.VMEM((GROUPS, n // 2, rows, GC), jnp.float32),
            pltpu.VMEM((GROUPS, n, 2 * GH, rows), jnp.float32),
            pltpu.VMEM((GROUPS, n, rows, GC), jnp.bfloat16),
            pltpu.VMEM((GROUPS, n, rows, GC), jnp.bfloat16),
            pltpu.VMEM((GROUPS, n, 2 * GH, rows), jnp.float32),
            pltpu.VMEM((rows, width), jnp.bfloat16),
            pltpu.SemaphoreType.DMA((steps, steps)),
            pltpu.SemaphoreType.DMA((steps, steps)),
            pltpu.SemaphoreType.DMA((GROUPS, steps)),
            pltpu.SemaphoreType.DMA((GROUPS, steps)),
            pltpu.SemaphoreType.DMA((GROUPS, steps)),
            pltpu.SemaphoreType.DMA((GROUPS, steps)),
        ],
        compiler_params=pltpu.CompilerParams(
            collective_id=0, has_side_effects=True, vmem_limit_bytes=56 * 2**20),
    )(queries, tokens, key_weight, value_weight, out_weight)


def solution(mesh):
    placed = (P("tok", None), P(("groups", "tok"), None), P(), P(), P())
    return jax.shard_map(
        program, mesh=mesh, in_specs=placed, out_specs=P(("groups", "tok"), None), check_vma=False
    )
```

```python
import functools
import math

import jax
import jax.numpy as jnp
from jax import lax
from jax.experimental import pallas as pl
from jax.experimental.pallas import tpu as pltpu
from jax.sharding import PartitionSpec as P

H = 16
HD = 64


epsilon = 1e-05


def layer_norm(matrix):
    widened = matrix.astype(jnp.float32)
    center = widened - jnp.mean(widened, axis=1, keepdims=True)
    spread = jnp.mean(center * center, axis=1, keepdims=True)
    return (center * lax.rsqrt(spread + epsilon)).astype(jnp.bfloat16)


def head_partials(gathered, key_rows, value_rows, head_index):
    first_col = head_index * HD
    head_query = lax.dynamic_slice_in_dim(gathered, first_col, HD, 1)
    head_keys = lax.dynamic_slice_in_dim(key_rows, first_col, HD, 1)
    head_values = lax.dynamic_slice_in_dim(value_rows, first_col, HD, 1)
    scores = lax.dot_general(
        head_query, head_keys, (((1,), (1,)), ((), ())), preferred_element_type=jnp.float32
    ) * HD ** (-0.5)
    row_max = jnp.max(scores, axis=1)
    weights = jnp.exp(scores - row_max[:, None])
    totals = jnp.sum(weights, axis=1)
    partial_value = jnp.dot(
        weights.astype(jnp.bfloat16), head_values, preferred_element_type=jnp.float32
    )
    return (row_max, totals, partial_value)


def on_device(queries, tokens, key_weight, value_weight, out_weight):
    tok_count = lax.axis_size("tok")
    gathered = lax.all_gather(queries, "tok", axis=0, tiled=True)
    normed = layer_norm(tokens)
    key_rows = jnp.dot(normed, key_weight, preferred_element_type=jnp.float32).astype(jnp.bfloat16)
    value_rows = jnp.dot(normed, value_weight, preferred_element_type=jnp.float32).astype(
        jnp.bfloat16
    )

    def one_head(head_index):
        return head_partials(gathered, key_rows, value_rows, head_index)

    head_max, head_total, head_out = lax.map(one_head, jnp.arange(H, dtype=jnp.int32))
    latent_count = gathered.shape[0]
    owned_rows = latent_count // tok_count
    row_max = jnp.transpose(head_max)
    totals = jnp.transpose(head_total)
    partial_value = jnp.transpose(head_out, (1, 0, 2)).reshape(latent_count, H * HD)
    global_max = lax.pmax(row_max.astype(jnp.bfloat16), "tok").astype(row_max.dtype)
    factor = jnp.exp(row_max - global_max)
    scaled_out = (partial_value.reshape(latent_count, H, HD) * factor[..., None]).reshape(
        latent_count, H * HD
    )
    summed_out, summed_total = (
        lax.psum_scatter(scaled_out, "tok", scatter_dimension=0, tiled=True),
        lax.psum_scatter(totals * factor, "tok", scatter_dimension=0, tiled=True),
    )
    summed_out = summed_out.reshape(owned_rows, H, HD)
    attended = (
        (summed_out / summed_total[..., None]).reshape(owned_rows, H * HD).astype(jnp.bfloat16)
    )
    return jnp.dot(attended, out_weight, preferred_element_type=jnp.float32).astype(jnp.bfloat16)


GROUPS = 4
GH = H // GROUPS
GC = GH * HD
PAIRS = H // 2
GP = GH // 2
CHUNKS = 4
EXPO = math.log2(math.e) * HD ** (-0.5)


def fused(n, q_in, x_in, wk_in, wv_in, wo_in, out_ref,
          x_ref, wk_ref, wv_ref, wo_ref, load_sem,
          q_ref, k_ref, v_ref, acc_ref, st_ref, sbuf, rbuf, rst,
          att_ref, qs_sem, qr_sem, os_sem, or_sem, ts_sem, tr_sem):
    steps = n.bit_length() - 1
    rows = q_in.shape[0]
    tokens = x_ref.shape[0]
    me = lax.axis_index("tok")
    bits = [n >> (s + 1) for s in range(steps)]

    def partner(bit):
        return me + bit - 2 * bit * lax.rem(me // bit, 2)

    loads = [
        pltpu.make_async_copy(src, dst, load_sem.at[i])
        for i, (src, dst) in enumerate(((x_in, x_ref), (wk_in, wk_ref), (wv_in, wv_ref), (wo_in, wo_ref)))]
    barrier = pltpu.get_barrier_semaphore()
    for bit in bits:
        pl.semaphore_signal(barrier, inc=1, device_id={"tok": partner(bit)}, device_id_type=pl.DeviceIdType.MESH)
    for load in loads:
        load.start()
    q_ref[0] = q_in[...]
    pl.semaphore_wait(barrier, steps)

    def gather(s, part):
        first = 0 if part == 0 else 1 << (part - 1)
        size = max(first, 1)
        return pltpu.make_async_remote_copy(
            src_ref=q_ref.at[pl.ds(first, size)], dst_ref=q_ref.at[pl.ds((1 << s) + first, size)],
            send_sem=qs_sem.at[s, part], recv_sem=qr_sem.at[s, part],
            device_id={"tok": partner(n >> (s + 1))}, device_id_type=pl.DeviceIdType.MESH)

    def arrived(k):
        for part in range(k + 1):
            gather(k, part).wait_recv()
        for s in range(k + 1, steps):
            gather(s, k + 1).start()

    def reduce_out(g, s):
        half = n >> (s + 1)
        return pltpu.make_async_remote_copy(
            src_ref=sbuf.at[g, pl.ds(half, half)], dst_ref=rbuf.at[g, pl.ds(half, half)],
            send_sem=os_sem.at[g, s], recv_sem=or_sem.at[g, s],
            device_id={"tok": partner(1 << s)}, device_id_type=pl.DeviceIdType.MESH)

    def reduce_stat(g, s):
        half = n >> (s + 1)
        return pltpu.make_async_remote_copy(
            src_ref=st_ref.at[g, pl.ds(half, half)], dst_ref=rst.at[g, pl.ds(half, half)],
            send_sem=ts_sem.at[g, s], recv_sem=tr_sem.at[g, s],
            device_id={"tok": partner(1 << s)}, device_id_type=pl.DeviceIdType.MESH)

    for s in range(steps):
        gather(s, 0).start()

    part = tokens // CHUNKS

    def project(c):
        first = c * part
        x = x_ref[pl.ds(first, part), :].astype(jnp.float32)
        center = x - jnp.mean(x, axis=1, keepdims=True)
        spread = jnp.mean(center * center, axis=1, keepdims=True)
        normed = (center * lax.rsqrt(spread + epsilon)).astype(jnp.bfloat16)
        ones = jnp.ones((part, 2 * HD), jnp.bfloat16)
        keys = jnp.dot(normed, wk_ref[...], preferred_element_type=jnp.float32).astype(jnp.bfloat16)
        for p in range(PAIRS):
            k_ref[p, pl.ds(first, part), :] = keys[:, p * 128 : (p + 1) * 128]
        values = jnp.dot(normed, wv_ref[...], preferred_element_type=jnp.float32).astype(jnp.bfloat16)
        for p in range(PAIRS):
            v_ref[p, pl.ds(first, part), 0:128] = values[:, p * 128 : (p + 1) * 128]
            v_ref[p, pl.ds(first, part), 128:256] = ones

    def project_some(first, last):
        @pl.loop(first, last)
        def _(c):
            project(c)

    for load in loads[:3]:
        load.wait()
    project_some(0, CHUNKS - 1)
    arrived(0)
    project_some(CHUNKS - 1, CHUNKS)
    arrived(1)

    quarter = n // 4
    chunk = quarter * rows
    lane = lax.broadcasted_iota(jnp.int32, (chunk, 128), 1)

    def attend(g, q):
        stats = jnp.zeros((chunk, 128), jnp.float32)
        for j in range(GP):
            pair = g * GP + j
            cols = pl.ds(pl.multiple_of(pair * 128, 128), 128)
            query = q_ref[pl.ds(q * quarter, quarter), :, cols].reshape(chunk, 128)
            zero = jnp.zeros_like(query)
            both = jnp.concatenate([jnp.where(lane < HD, query, zero), jnp.where(lane < HD, zero, query)], axis=0)
            scores = lax.dot_general(both, k_ref[pair], (((1,), (1,)), ((), ())), preferred_element_type=jnp.float32)
            top = jnp.max(scores, axis=1, keepdims=True)
            weights = jnp.exp2((scores - top) * EXPO).astype(jnp.bfloat16)
            product = jnp.dot(weights, v_ref[pair], preferred_element_type=jnp.float32)
            merged = jnp.where(lane < HD, product[:chunk, :128], product[chunk:, :128]).reshape(quarter, rows, 128)
            where = slice(j * 128, (j + 1) * 128)
            if q < 2:
                acc_ref[g, pl.ds(q * quarter, quarter), :, where] = merged
            else:
                sbuf[g, pl.ds(q * quarter, quarter), :, where] = merged.astype(jnp.bfloat16)
            for e in range(2):
                mine = slice(e * chunk, (e + 1) * chunk)
                stats = jnp.where(lane == 2 * j + e, top[mine], stats)
                stats = jnp.where(lane == GH + 2 * j + e, product[mine, 128:], stats)
        for b in range(quarter):
            turned = stats[b * rows : (b + 1) * rows].T
            st_ref[g, q * quarter + b] = turned[: 2 * GH]

    narrow = lax.broadcasted_iota(jnp.int32, (rows, 128), 1) < HD

    def spread_heads(turned):
        return jnp.concatenate(
            [jnp.where(narrow, turned[:, 2 * j : 2 * j + 1], turned[:, 2 * j + 1 : 2 * j + 2]) for j in range(GP)], axis=1)

    def combine(g, s):
        half = n >> (s + 1)
        reduce_out(g, s).wait_recv()
        reduce_stat(g, s).wait_recv()

        def one(b):
            own, other = st_ref[g, b], rst[g, half + b]
            top = jnp.maximum(own[:GH], other[:GH])
            f_own = jnp.exp2((own[:GH] - top) * EXPO)
            f_other = jnp.exp2((other[:GH] - top) * EXPO)
            total = own[GH:] * f_own + other[GH:] * f_other
            st_ref[g, b] = jnp.concatenate([top, total], axis=0)
            turned = jnp.concatenate([f_own, f_other], axis=0).T
            summed = (acc_ref[g, b] * spread_heads(turned[:, :GH])
                      + rbuf[g, half + b].astype(jnp.float32) * spread_heads(turned[:, GH:]))
            return summed

        for b in range(half):
            summed = one(b)
            if b >= half // 2 and half > 1:
                sbuf[g, b] = summed.astype(jnp.bfloat16)
            else:
                acc_ref[g, b] = summed
        if s + 1 < steps:
            reduce_out(g, s + 1).start()
            reduce_stat(g, s + 1).start()

    @pl.loop(0, GROUPS)
    def _(g):
        attend(g, 0)

    arrived(2)

    @pl.loop(0, GROUPS - 1)
    def _(g):
        attend(g, 1)

    arrived(3)

    @pl.loop(0, GROUPS)
    def _(g):
        attend(g, 2)
        attend(g, 3)
        reduce_out(g, 0).start()
        reduce_stat(g, 0).start()
        for s in reversed(range(min(steps, GROUPS - 1))):
            @pl.when(g > s)
            def _():
                combine(g - 1 - s, s)

    attend(GROUPS - 1, 1)
    for t in range(GROUPS, GROUPS + steps):
        for s in range(steps):
            if 0 <= t - 1 - s < GROUPS:
                combine(t - 1 - s, s)

    for g in range(GROUPS):
        share = spread_heads(st_ref[g, 0].T[:, GH:])
        att_ref[:, g * GC : (g + 1) * GC] = (acc_ref[g, 0] / share).astype(jnp.bfloat16)
    loads[3].wait()
    out_ref[...] = jnp.dot(att_ref[...], wo_ref[...], preferred_element_type=jnp.float32).astype(out_ref.dtype)

    for s in range(steps):
        for part in range(s + 1):
            gather(s, part).wait_send()

    @pl.loop(0, GROUPS)
    def _(g):
        for s in range(steps):
            reduce_out(g, s).wait_send()
            reduce_stat(g, s).wait_send()


def program(queries, tokens, key_weight, value_weight, out_weight):
    n = lax.axis_size("tok")
    rows, width = queries.shape
    count = tokens.shape[0]
    if n != 16 or rows % 16 or count % 1024 or width != H * HD:
        return on_device(queries, tokens, key_weight, value_weight, out_weight)
    vmem = pl.BlockSpec(memory_space=pltpu.VMEM)
    steps = n.bit_length() - 1
    return pl.pallas_call(
        functools.partial(fused, n),
        out_shape=jax.ShapeDtypeStruct((rows, width), jnp.bfloat16),
        in_specs=[vmem] + [pl.BlockSpec(memory_space=pl.ANY)] * 4,
        out_specs=vmem,
        scratch_shapes=[
            pltpu.VMEM(tokens.shape, tokens.dtype),
            pltpu.VMEM(key_weight.shape, key_weight.dtype),
            pltpu.VMEM(value_weight.shape, value_weight.dtype),
            pltpu.VMEM(out_weight.shape, out_weight.dtype),
            pltpu.SemaphoreType.DMA((4,)),
            pltpu.VMEM((n, rows, width), jnp.bfloat16),
            pltpu.VMEM((PAIRS, count, 128), jnp.bfloat16),
            pltpu.VMEM((PAIRS, count, 256), jnp.bfloat16),
            pltpu.VMEM((GROUPS, n // 2, rows, GC), jnp.float32),
            pltpu.VMEM((GROUPS, n, 2 * GH, rows), jnp.float32),
            pltpu.VMEM((GROUPS, n, rows, GC), jnp.bfloat16),
            pltpu.VMEM((GROUPS, n, rows, GC), jnp.bfloat16),
            pltpu.VMEM((GROUPS, n, 2 * GH, rows), jnp.float32),
            pltpu.VMEM((rows, width), jnp.bfloat16),
            pltpu.SemaphoreType.DMA((steps, steps)),
            pltpu.SemaphoreType.DMA((steps, steps)),
            pltpu.SemaphoreType.DMA((GROUPS, steps)),
            pltpu.SemaphoreType.DMA((GROUPS, steps)),
            pltpu.SemaphoreType.DMA((GROUPS, steps)),
            pltpu.SemaphoreType.DMA((GROUPS, steps)),
        ],
        compiler_params=pltpu.CompilerParams(
            collective_id=0, has_side_effects=True, vmem_limit_bytes=56 * 2**20),
    )(queries, tokens, key_weight, value_weight, out_weight)


def solution(mesh):
    placed = (P("tok", None), P(("groups", "tok"), None), P(), P(), P())
    return jax.shard_map(
        program, mesh=mesh, in_specs=placed, out_specs=P(("groups", "tok"), None), check_vma=False
    )
```
